32 devices in a mesh: parts: 2 (over y), frag: 8 (over z, x), orb: 2 (over core).
Axes of the slice: x: 2, y: 2, z: 4, core: 2. Of those that a mesh axis runs over, the one named last changes fastest.
Arguments:
- potential: float32 [128, 768], P(('parts', 'frag')), parts along dimension 0, may hold values from -1 to 1
- orbitals: bfloat16 [16, 128, 4096], P(('parts', 'frag'), None, 'orb'), parts along dimension 0, may hold values from -6 to 6
- offsets: int32 [16, 3], P('parts'), parts along dimension 0, may hold values from 0 to 56, as said below
- weight_signs: int32 [16], P('parts'), parts along dimension 0, may hold values from -1 to 1, as said below
- assignment: int32 [16], P('parts'), parts along dimension 0, may hold values from 0 to 7, each once
Outputs:
- density: float32 [128, 768], P(('parts', 'frag')), parts along dimension 0
- orbitals_out: float32 [16, 128, 4096], P(('parts', 'frag'), None, 'orb'), parts along dimension 0
The draws below stay inside these ranges and needn't reach their ends.
There are 2 independent parts, one for each index of `parts`. The reference program is written for one: setup_inputs(seed, part) draws one part's arguments, and reference() takes and returns one part's arrays. A program takes and returns all parts, laid end to end along the dimension named above; each array names one. Nothing has to cross between parts.
Inputs may be any that keep to these rules, and one draw needn't show every extreme that they name: offsets[f] = (oz, ox, oy): oz is 8 times a slab number below 8, ox is 0 or 8, oy is 0, 8 or 16; some fragment lies on the last slab with corner (8, 16) in x and y, and some fragment has ox = 0. `weight_signs`: each entry is -1 or 1.
All inputs are finite; a program needn't handle non-finite values.
Results may differ from the reference program's by a relative error of at most 0.0003.
Values sent between devices are 32-bit elements; how exact they have to be, the bound alone decides.
A program may use at most 64 MiB of HBM per device.

```python
import jax
import jax.numpy as jnp
from jax import lax

NORB = 128
FSIDE = 16
DEGREE = 8
PASSES = 3
SLAB = 8
PLANE = 256
FCELLS = 4096
GX = 24
GY = 32
NFRAG = 8
GZ = 64


def draw_potential(key, part):
    key = jax.random.fold_in(key, 37)
    key_a, key_b, key_c = jax.random.split(key, 3)
    rough = jax.random.uniform(key_a, (GZ, GX * GY), jnp.float32, -1.0, 1.0)
    noise = jax.random.uniform(key_b, (GZ, GX * GY), jnp.float32, -1.0, 1.0)
    extra_slab = jax.random.randint(key_c, (), 0, NFRAG)
    slab_of_row = lax.broadcasted_iota(jnp.int32, (GZ, 1), 0) // SLAB
    in_well = (slab_of_row == 0) | (slab_of_row == extra_slab)
    well = -0.75 + 0.25 * noise
    return jnp.where(in_well, well, rough).astype(jnp.float32)


def draw_offsets(key, part):
    key = jax.random.fold_in(key, 11)
    key_a, key_b, key_c, key_d, key_e = jax.random.split(key, 5)
    first = jax.random.randint(key_a, (NFRAG,), 0, NFRAG)
    second = jax.random.randint(key_b, (NFRAG,), 0, NFRAG)
    slab_number = jnp.minimum(first, second)
    corner_x = jax.random.randint(key_c, (NFRAG,), 0, 2)
    corner_y = jax.random.randint(key_d, (NFRAG,), 0, 3)
    chosen = jax.random.randint(key_e, (), 0, NFRAG)
    following = (chosen + 1) % NFRAG
    index_all = lax.broadcasted_iota(jnp.int32, (NFRAG,), 0)
    is_chosen = index_all == chosen
    slab_number = jnp.where(is_chosen, NFRAG - 1, slab_number)
    corner_x = jnp.where(is_chosen, 1, jnp.where(index_all == following, 0, corner_x))
    corner_y = jnp.where(is_chosen, 2, corner_y)
    return jnp.stack([slab_number * SLAB, corner_x * SLAB, corner_y * SLAB], axis=1).astype(jnp.int32)


def draw_weight_signs(key, part):
    key = jax.random.fold_in(key, 23)
    return (2 * jax.random.randint(key, (NFRAG,), 0, 2) - 1).astype(jnp.int32)


def steps_of(stream_key, shape, cuts, smallest, top_value):
    level, own = 1.0, jax.random.fold_in(stream_key, 6)
    for position, shards_of in cuts:
        heights = jnp.exp(jax.random.uniform(jax.random.fold_in(own, position), (shards_of,), jnp.float32, smallest / len(cuts), top_value / len(cuts)))
        level = level * jnp.repeat(heights, shape[position] // shards_of).reshape([-1 if axis == position else 1 for axis in range(len(shape))])
    return level


def normal_values(stream_key, extent, width, most, pieces=(), kind=jnp.bfloat16):
    entries = width * jax.random.normal(stream_key, extent, jnp.float32)
    if pieces:
        entries = entries * steps_of(stream_key, extent, pieces, -0.22, 0.18)
    return jnp.clip(entries, -most, most).astype(kind)


def setup_inputs(seed: int = 0, part: int = 0) -> dict:
    splits = jax.random.split(jax.random.key(seed), 6)
    own_keys = jax.random.split(jax.random.fold_in(splits[5], part), 6)
    return {
        "potential": draw_potential(jax.random.fold_in(jax.random.fold_in(splits[5], part), 71), part),
        "orbitals": normal_values(own_keys[1], (NFRAG, NORB, FCELLS), 1.0, 6.0, ((0, 8), (2, 2))),
        "offsets": draw_offsets(jax.random.fold_in(jax.random.fold_in(splits[5], part), 71), part),
        "weight_signs": draw_weight_signs(jax.random.fold_in(jax.random.fold_in(splits[5], part), 71), part),
        "assignment": jax.random.permutation(own_keys[4], NFRAG).astype(jnp.int32),
    }


SPECTRUM_MID = 3.5
SPECTRUM_HALF = 3.75
OCCUPY_SLOPE = 0.2

def plane_sum(states, side_len):
    plane_len = states.shape[-1]
    pads = [(0, 0)] * (states.ndim - 1) + [(side_len, side_len)]
    padded = jnp.pad(states, pads)
    summed = padded[..., 2 * side_len:] + padded[..., :plane_len]
    column = lax.broadcasted_iota(jnp.int32, (plane_len,), 0) % side_len
    y_after = padded[..., side_len + 1:side_len + 1 + plane_len]
    y_before = padded[..., side_len - 1:side_len - 1 + plane_len]
    zero_val = jnp.zeros_like(y_after)
    return summed + jnp.where(column < side_len - 1, y_after, zero_val) + jnp.where(column > 0, y_before, zero_val)

def hamiltonian(padded, local_potential, side_len):
    centre = padded[:, 1:-1]
    neighbours = padded[:, 2:] + padded[:, :-2] + plane_sum(centre, side_len)
    return (3.0 + local_potential) * centre - 0.5 * neighbours

def chebyshev(states, operate):
    previous = states
    current = (operate(states) - SPECTRUM_MID * states) / SPECTRUM_HALF
    for repeat in range(DEGREE - 1):
        following = 2.0 * (operate(current) - SPECTRUM_MID * current) / SPECTRUM_HALF - previous
        previous, current = (current, following)
    return current

def gram(left, right):
    rows_left = left.reshape(left.shape[0], -1)
    rows_right = right.reshape(right.shape[0], -1)
    product = jnp.dot(rows_left.astype(jnp.float32), rows_right.T.astype(jnp.float32), precision=lax.Precision.HIGHEST, preferred_element_type=jnp.float32)
    return product / FCELLS

def orthonormal(matrix, states):
    lower = jnp.linalg.cholesky(matrix)
    flat = states.reshape(states.shape[0], -1)
    solved = lax.linalg.triangular_solve(lower, flat, left_side=True, lower=True)
    return (solved.reshape(states.shape), lower)

def occupation(projected):
    order_len = projected.shape[0]
    eye_mat = jnp.eye(order_len, dtype=jnp.float32)
    shifted = projected - jnp.trace(projected) / order_len * eye_mat
    occupied = 0.5 * eye_mat - OCCUPY_SLOPE * shifted
    for repeat in range(2):
        square = jnp.dot(occupied.astype(jnp.float32), occupied.astype(jnp.float32), precision=lax.Precision.HIGHEST, preferred_element_type=jnp.float32)
        cube = jnp.dot(square.astype(jnp.float32), occupied.astype(jnp.float32), precision=lax.Precision.HIGHEST, preferred_element_type=jnp.float32)
        occupied = 3.0 * square - 2.0 * cube
    return occupied

def fragment_density(states, occupied, sign_val):
    flat = states.reshape(states.shape[0], -1)
    mixed = jnp.dot(occupied.astype(jnp.float32), flat.astype(jnp.float32), precision=lax.Precision.HIGHEST, preferred_element_type=jnp.float32)
    return sign_val * jnp.sum(flat * mixed, axis=0) / NORB

def reference(potential, orbitals, offsets, weight_signs, assignment):
    total_rows = potential.shape[0]
    grid = potential.reshape(total_rows, GX, GY)

    def one_slot(inputs):
        states_in, fragment = inputs
        place = offsets[fragment]
        zero_idx = place[0] * 0
        rolled = jnp.roll(grid, -place[0], axis=0)[:FSIDE]
        local_potential = lax.dynamic_slice(rolled, (zero_idx, place[1], place[2]), (FSIDE, FSIDE, FSIDE)).reshape(FSIDE, PLANE)
        states = states_in.astype(jnp.float32).reshape(NORB, FSIDE, PLANE)

        def operate(field_now):
            return hamiltonian(jnp.pad(field_now, ((0, 0), (1, 1), (0, 0))), local_potential, FSIDE)
        for repeat in range(PASSES):
            filtered = chebyshev(states, operate)
            states, lower = orthonormal(gram(filtered, filtered), filtered)
        coupling = gram(states, operate(states))
        projected = 0.5 * (coupling + coupling.T)
        occupied = occupation(projected)
        density = fragment_density(states, occupied, weight_signs[fragment].astype(jnp.float32))
        return (states.reshape(NORB, FCELLS), density.reshape(FSIDE, FSIDE, FSIDE))
    states_all, densities = lax.map(one_slot, (orbitals, assignment))

    def add_one(summed, inputs):
        density, fragment = inputs
        place = offsets[fragment]
        zero_idx = place[0] * 0
        placed = lax.dynamic_update_slice(jnp.zeros((FSIDE, GX, GY), jnp.float32), density, (zero_idx, place[1], place[2]))
        full = jnp.zeros((total_rows, GX * GY), jnp.float32).at[:FSIDE].set(placed.reshape(FSIDE, GX * GY))
        return (summed + jnp.roll(full, place[0], axis=0), None)
    density_sum, unused = lax.scan(add_one, jnp.zeros((total_rows, GX * GY), jnp.float32), (densities, assignment))
    return (density_sum, states_all)
```

```python
import jax
import jax.numpy as jnp
from jax import lax
from jax.experimental import pallas as pl
from jax.experimental.pallas import tpu as pltpu
from jax.sharding import PartitionSpec as P

NORB = 128
FSIDE = 16
DEGREE = 8
PASSES = 3
SLAB = 8
PLANE = 256
FCELLS = 4096
GX = 24
GY = 32
PAD = FSIDE + 2
ROWS = 32
LOW = 8

SPECTRUM_MID = 3.5
SPECTRUM_HALF = 3.75
OCCUPY_SLOPE = 0.2
COUPLE = 1.0 / SPECTRUM_HALF
HIGHEST = lax.Precision.HIGHEST


def dot(left, right, dims):
    return lax.dot_general(
        left, right, (dims, ((), ())), precision=HIGHEST, preferred_element_type=jnp.float32
    )


def inverse_factor(matrix):
    panels = NORB // 8
    lane = lax.broadcasted_iota(jnp.int32, (8, NORB), 1)
    sub = lax.broadcasted_iota(jnp.int32, (8, NORB), 0)
    a = [matrix[8 * i : 8 * i + 8] for i in range(panels)]
    w = [jnp.where(lane == sub + 8 * i, 1.0, 0.0).astype(jnp.float32) for i in range(panels)]
    out = []

    def row(x, j):
        return jnp.broadcast_to(x[j : j + 1], (8, NORB))

    for k in range(panels):
        cols = {
            i: [jnp.broadcast_to(a[i][:, 8 * k + j : 8 * k + j + 1], (8, NORB)) for j in range(8)]
            for i in range(k, panels)
        }
        scale = jnp.zeros((8, NORB), jnp.float32)
        for j in range(8):
            root = lax.rsqrt(row(cols[k][j], j))
            inv = root * root
            scale = jnp.where(sub == j, root, scale)
            col_rows = [row(cols[k][l], j) * inv for l in range(j + 1, 8)]
            a_row = row(a[k], j) * inv
            w_row = row(w[k], j) * inv
            for i in range(k, panels):
                f = cols[i][j]
                if i == k:
                    f = jnp.where(sub > j, f, 0.0)
                for l in range(j + 1, 8):
                    cols[i][l] = cols[i][l] - f * col_rows[l - j - 1]
                a[i] = a[i] - f * a_row
                w[i] = w[i] - f * w_row
        out.append(w[k] * scale)
    return jnp.concatenate(out, axis=0)


def fragment_kernel(orb_ref, own_ref, other_ref, v_ref, states_ref, rho_ref, xa, xb, w_ref):
    orb = orb_ref[0]

    def clear(z, _):
        xa[z] = jnp.zeros((PAD, ROWS, NORB), jnp.float32)
        xb[z] = jnp.zeros((PAD, ROWS, NORB), jnp.float32)
        return 0

    lax.fori_loop(0, PAD, clear, 0)

    for z in range(SLAB):
        block = own_ref[:, PLANE * z : PLANE * (z + 1)].astype(jnp.float32).T
        xa[orb * SLAB + z + 1, 1 : FSIDE + 1, LOW : LOW + FSIDE, :] = block.reshape(FSIDE, FSIDE, NORB)
        block = other_ref[:, PLANE * z : PLANE * (z + 1)].T
        xa[(1 - orb) * SLAB + z + 1, 1 : FSIDE + 1, LOW : LOW + FSIDE, :] = block.reshape(FSIDE, FSIDE, NORB)

    mid = pl.ds(LOW, FSIDE)

    def stencil(src, z, x):
        c = src[z + 1, x + 1, mid, :]
        n = src[z, x + 1, mid, :] + src[z + 2, x + 1, mid, :]
        n = n + (src[z + 1, x, mid, :] + src[z + 1, x + 2, mid, :])
        n = n + (src[z + 1, x + 1, pl.ds(LOW - 1, FSIDE), :] + src[z + 1, x + 1, pl.ds(LOW + 1, FSIDE), :])
        return v_ref[z, x] * c - COUPLE * n

    def first(src, dst):
        def body(z, _):
            for x in range(FSIDE):
                dst[z + 1, x + 1, mid, :] = 0.5 * stencil(src, z, x)
            return 0

        lax.fori_loop(0, FSIDE, body, 0)

    def later(src, dst):
        def body(z, _):
            for x in range(FSIDE):
                dst[z + 1, x + 1, mid, :] = stencil(src, z, x) - dst[z + 1, x + 1, mid, :]
            return 0

        lax.fori_loop(0, FSIDE, body, 0)

    def plane(src, z):
        return src[z + 1, 1 : FSIDE + 1, mid, :].reshape(PLANE, NORB)

    def one_pass(_, carry):
        first(xa, xb)
        later(xb, xa)

        def pair(_, c):
            later(xa, xb)
            later(xb, xa)
            return c

        lax.fori_loop(0, DEGREE // 2 - 1, pair, 0)

        def add(z, total):
            y = plane(xa, z)
            return total + dot(y, y, ((0,), (0,)))

        total = lax.fori_loop(0, FSIDE, add, jnp.zeros((NORB, NORB), jnp.float32))
        w_ref[...] = inverse_factor(total / FCELLS)

        def apply(z, c):
            s = dot(plane(xa, z), w_ref[...], ((1,), (1,)))
            xa[z + 1, 1 : FSIDE + 1, mid, :] = s.reshape(FSIDE, FSIDE, NORB)
            return c

        lax.fori_loop(0, FSIDE, apply, 0)
        return carry

    lax.fori_loop(0, PASSES, one_pass, 0)

    def couple(z, total):
        parts = []
        for x in range(FSIDE):
            parts.append((SPECTRUM_HALF / 2) * stencil(xa, z, x) + SPECTRUM_MID * xa[z + 1, x + 1, mid, :])
        h = jnp.concatenate(parts, axis=0)
        return total + dot(plane(xa, z), h, ((0,), (0,)))

    coupling = lax.fori_loop(0, FSIDE, couple, jnp.zeros((NORB, NORB), jnp.float32)) / FCELLS
    projected = 0.5 * (coupling + coupling.T)
    rows = lax.broadcasted_iota(jnp.int32, (NORB, NORB), 0)
    columns = lax.broadcasted_iota(jnp.int32, (NORB, NORB), 1)
    eye = jnp.where(rows == columns, 1.0, 0.0).astype(jnp.float32)
    trace = jnp.sum(projected * eye)
    occupied = 0.5 * eye - OCCUPY_SLOPE * (projected - trace / NORB * eye)
    for _ in range(2):
        square = dot(occupied, occupied, ((1,), (0,)))
        cube = dot(square, occupied, ((1,), (0,)))
        occupied = 3.0 * square - 2.0 * cube
    w_ref[...] = occupied
    ones = jnp.ones((8, NORB), jnp.float32)

    def density(z, c):
        s = plane(xa, z)
        m = s * dot(s, w_ref[...], ((1,), (0,)))
        r = dot(ones, m, ((1,), (1,)))
        rho_ref[pl.ds(z, 1), :] = r[0:1]
        return c

    lax.fori_loop(0, FSIDE, density, 0)
    for z in range(SLAB):
        states_ref[:, PLANE * z : PLANE * (z + 1)] = plane(xa, orb * SLAB + z).T


def local(potential, orbitals, offsets, weight_signs, assignment):
    frag_count = lax.axis_size("frag")
    slot_index = lax.axis_index("frag")
    orb_index = lax.axis_index("orb")
    own = orbitals[0]
    other = lax.ppermute(own.astype(jnp.float32), "orb", [(0, 1), (1, 0)])
    place = offsets[assignment[slot_index]]
    zero_idx = place[0] * 0
    piece = lax.all_gather(potential, "frag", axis=0, tiled=True)
    piece = jnp.concatenate([piece, piece[:SLAB]], axis=0).reshape(-1, GX, GY)
    v = lax.dynamic_slice(piece, (place[0], place[1], place[2]), (FSIDE, FSIDE, FSIDE))
    v = (v + (3.0 - SPECTRUM_MID)) * (2.0 / SPECTRUM_HALF)
    v = jnp.broadcast_to(v[..., None], (FSIDE, FSIDE, FSIDE, NORB))
    vmem = pl.BlockSpec(memory_space=pltpu.VMEM)
    states, rho = pl.pallas_call(
        fragment_kernel,
        out_shape=(
            jax.ShapeDtypeStruct((NORB, SLAB * PLANE), jnp.float32),
            jax.ShapeDtypeStruct((FSIDE, PLANE), jnp.float32),
        ),
        in_specs=[pl.BlockSpec(memory_space=pltpu.SMEM), vmem, vmem, vmem],
        out_specs=(vmem, vmem),
        scratch_shapes=[
            pltpu.VMEM((PAD, PAD, ROWS, NORB), jnp.float32),
            pltpu.VMEM((PAD, PAD, ROWS, NORB), jnp.float32),
            pltpu.VMEM((NORB, NORB), jnp.float32),
        ],
        compiler_params=pltpu.CompilerParams(vmem_limit_bytes=40 * 1024 * 1024),
    )(orb_index.reshape(1), own, other, v)

    rho_all = lax.all_gather(rho, "frag", axis=0)
    places = offsets[assignment]
    signs = weight_signs[assignment].astype(jnp.float32) / NORB
    half = (slot_index - places[:, 0] // SLAB) % frag_count
    lands = half[:, None] == jnp.arange(2)[None, :]
    variant = (places[:, 1] // SLAB) * 3 + places[:, 2] // SLAB
    weights = jnp.where(
        lands[None] & (variant[None, :, None] == jnp.arange(6)[:, None, None]), signs[None, :, None], 0.0
    )
    summed = jnp.dot(
        weights.reshape(6, 2 * frag_count),
        rho_all.reshape(2 * frag_count, SLAB * PLANE),
        precision=HIGHEST,
        preferred_element_type=jnp.float32,
    ).reshape(6, SLAB, FSIDE, FSIDE)
    density = jnp.zeros((SLAB, GX, GY), jnp.float32)
    for i in range(6):
        ox, oy = 8 * (i // 3), 8 * (i % 3)
        density = density + jnp.pad(summed[i], ((0, 0), (ox, GX - FSIDE - ox), (oy, GY - FSIDE - oy)))
    return (density.reshape(SLAB, GX * GY), states[None])


def solution(mesh):
    return jax.shard_map(
        local,
        mesh=mesh,
        in_specs=(
            P(("parts", "frag"), None),
            P(("parts", "frag"), None, "orb"),
            P("parts", None),
            P("parts"),
            P("parts"),
        ),
        out_specs=(P(("parts", "frag"), None), P(("parts", "frag"), None, "orb")),
        check_vma=False,
    )
```

```python
import functools

import jax
import jax.numpy as jnp
from jax import lax
from jax.experimental import pallas as pl
from jax.experimental.pallas import tpu as pltpu
from jax.sharding import PartitionSpec as P

NORB = 128
FSIDE = 16
DEGREE = 8
PASSES = 3
SLAB = 8
PLANE = 256
FCELLS = 4096
GX = 24
GY = 32
PAD = FSIDE + 2
ROWS = 32
LOW = 8

SPECTRUM_MID = 3.5
SPECTRUM_HALF = 3.75
OCCUPY_SLOPE = 0.2
COUPLE = 1.0 / SPECTRUM_HALF
HIGHEST = lax.Precision.HIGHEST


def dot(left, right, dims):
    return lax.dot_general(
        left, right, (dims, ((), ())), precision=HIGHEST, preferred_element_type=jnp.float32
    )


def inverse_factor(matrix):
    panels = NORB // 8
    lane = lax.broadcasted_iota(jnp.int32, (8, NORB), 1)
    sub = lax.broadcasted_iota(jnp.int32, (8, NORB), 0)
    a = [matrix[8 * i : 8 * i + 8] for i in range(panels)]
    w = [jnp.where(lane == sub + 8 * i, 1.0, 0.0).astype(jnp.float32) for i in range(panels)]
    out = []

    def row(x, j):
        return jnp.broadcast_to(x[j : j + 1], (8, NORB))

    for k in range(panels):
        cols = {
            i: [jnp.broadcast_to(a[i][:, 8 * k + j : 8 * k + j + 1], (8, NORB)) for j in range(8)]
            for i in range(k, panels)
        }
        scale = jnp.zeros((8, NORB), jnp.float32)
        for j in range(8):
            root = lax.rsqrt(row(cols[k][j], j))
            inv = root * root
            scale = jnp.where(sub == j, root, scale)
            col_rows = [row(cols[k][l], j) * inv for l in range(j + 1, 8)]
            a_row = row(a[k], j) * inv
            w_row = row(w[k], j) * inv
            for i in range(k, panels):
                f = cols[i][j]
                if i == k:
                    f = jnp.where(sub > j, f, 0.0)
                for l in range(j + 1, 8):
                    cols[i][l] = cols[i][l] - f * col_rows[l - j - 1]
                a[i] = a[i] - f * a_row
                w[i] = w[i] - f * w_row
        out.append(w[k] * scale)
    return jnp.concatenate(out, axis=0)


def fragment_kernel(
    offsets_ref, assign_ref, own_ref, other_ref, pot_ref, states_ref, rho_ref, xa, xb, v_ref, turned, w_ref
):
    orb = lax.axis_index("orb")
    frag_count = pot_ref.shape[0]
    f = assign_ref[lax.axis_index("frag")]
    oz, ox, oy = offsets_ref[f, 0], offsets_ref[f, 1], offsets_ref[f, 2]
    for half in range(2):
        slab = pot_ref[lax.rem(oz // SLAB + half, frag_count)]
        turned[half] = ((slab + (3.0 - SPECTRUM_MID)) * (2.0 / SPECTRUM_HALF)).T
    for half in range(2):
        for x in range(FSIDE):
            cells = turned[half, pl.ds(pl.multiple_of((ox + x) * GY + oy, 8), FSIDE), :]
            for z in range(SLAB):
                v_ref[half * SLAB + z, x] = jnp.broadcast_to(cells[:, z : z + 1], (FSIDE, NORB))

    def clear(z, _):
        xa[z] = jnp.zeros((PAD, ROWS, NORB), jnp.float32)
        xb[z] = jnp.zeros((PAD, ROWS, NORB), jnp.float32)
        return 0

    lax.fori_loop(0, PAD, clear, 0)

    for z in range(SLAB):
        block = own_ref[:, PLANE * z : PLANE * (z + 1)].astype(jnp.float32).T
        xa[orb * SLAB + z + 1, 1 : FSIDE + 1, LOW : LOW + FSIDE, :] = block.reshape(FSIDE, FSIDE, NORB)
        block = other_ref[:, PLANE * z : PLANE * (z + 1)].T
        xa[(1 - orb) * SLAB + z + 1, 1 : FSIDE + 1, LOW : LOW + FSIDE, :] = block.reshape(FSIDE, FSIDE, NORB)

    mid = pl.ds(LOW, FSIDE)

    def stencil(src, z, x):
        c = src[z + 1, x + 1, mid, :]
        n = src[z, x + 1, mid, :] + src[z + 2, x + 1, mid, :]
        n = n + (src[z + 1, x, mid, :] + src[z + 1, x + 2, mid, :])
        n = n + (src[z + 1, x + 1, pl.ds(LOW - 1, FSIDE), :] + src[z + 1, x + 1, pl.ds(LOW + 1, FSIDE), :])
        return v_ref[z, x] * c - COUPLE * n

    def first(src, dst):
        def body(z, _):
            for x in range(FSIDE):
                dst[z + 1, x + 1, mid, :] = 0.5 * stencil(src, z, x)
            return 0

        lax.fori_loop(0, FSIDE, body, 0)

    def later(src, dst):
        def body(z, _):
            for x in range(FSIDE):
                dst[z + 1, x + 1, mid, :] = stencil(src, z, x) - dst[z + 1, x + 1, mid, :]
            return 0

        lax.fori_loop(0, FSIDE, body, 0)

    def plane(src, z):
        return src[z + 1, 1 : FSIDE + 1, mid, :].reshape(PLANE, NORB)

    def one_pass(_, carry):
        first(xa, xb)
        later(xb, xa)

        def pair(_, c):
            later(xa, xb)
            later(xb, xa)
            return c

        lax.fori_loop(0, DEGREE // 2 - 1, pair, 0)

        def add(z, total):
            y = plane(xa, z)
            return total + dot(y, y, ((0,), (0,)))

        total = lax.fori_loop(0, FSIDE, add, jnp.zeros((NORB, NORB), jnp.float32))
        w_ref[...] = inverse_factor(total / FCELLS)

        def apply(z, c):
            s = dot(plane(xa, z), w_ref[...], ((1,), (1,)))
            xa[z + 1, 1 : FSIDE + 1, mid, :] = s.reshape(FSIDE, FSIDE, NORB)
            return c

        lax.fori_loop(0, FSIDE, apply, 0)
        return carry

    lax.fori_loop(0, PASSES, one_pass, 0)

    def couple(z, total):
        parts = []
        for x in range(FSIDE):
            parts.append((SPECTRUM_HALF / 2) * stencil(xa, z, x) + SPECTRUM_MID * xa[z + 1, x + 1, mid, :])
        h = jnp.concatenate(parts, axis=0)
        return total + dot(plane(xa, z), h, ((0,), (0,)))

    coupling = lax.fori_loop(0, FSIDE, couple, jnp.zeros((NORB, NORB), jnp.float32)) / FCELLS
    projected = 0.5 * (coupling + coupling.T)
    rows = lax.broadcasted_iota(jnp.int32, (NORB, NORB), 0)
    columns = lax.broadcasted_iota(jnp.int32, (NORB, NORB), 1)
    eye = jnp.where(rows == columns, 1.0, 0.0).astype(jnp.float32)
    trace = jnp.sum(projected * eye)
    occupied = 0.5 * eye - OCCUPY_SLOPE * (projected - trace / NORB * eye)
    for _ in range(2):
        square = dot(occupied, occupied, ((1,), (0,)))
        cube = dot(square, occupied, ((1,), (0,)))
        occupied = 3.0 * square - 2.0 * cube
    w_ref[...] = occupied
    ones = jnp.ones((8, NORB), jnp.float32)

    def density(z, c):
        s = plane(xa, z)
        m = s * dot(s, w_ref[...], ((1,), (0,)))
        r = dot(ones, m, ((1,), (1,)))
        rho_ref[pl.ds(z, 1), :] = r[0:1]
        return c

    lax.fori_loop(0, FSIDE, density, 0)
    for z in range(SLAB):
        states_ref[:, PLANE * z : PLANE * (z + 1)] = plane(xa, orb * SLAB + z).T


def peer(**where):
    return {"device_id": where, "device_id_type": pl.DeviceIdType.MESH}


def greet(frag_count, with_orb):
    me, orb = lax.axis_index("frag"), lax.axis_index("orb")
    barrier = pltpu.get_barrier_semaphore()

    def hello(i, c):
        pl.semaphore_signal(barrier, inc=1, **peer(frag=lax.rem(me + i, frag_count)))
        return c

    lax.fori_loop(1, frag_count, hello, 0)
    if with_orb:
        pl.semaphore_signal(barrier, inc=1, **peer(orb=1 - orb))
    pl.semaphore_wait(barrier, frag_count - 1 + int(with_orb))


def spread(frag_count, source, gathered, send_sem, recv_sem):
    me = lax.axis_index("frag")

    def copy_to(i):
        return pltpu.make_async_remote_copy(
            src_ref=source,
            dst_ref=gathered.at[me],
            send_sem=send_sem.at[i - 1],
            recv_sem=recv_sem.at[i - 1],
            **peer(frag=lax.rem(me + i, frag_count)),
        )

    def start(i, c):
        copy_to(i).start()
        return c

    def wait(i, c):
        copy_to(i).wait()
        return c

    lax.fori_loop(1, frag_count, start, 0)
    return lambda: lax.fori_loop(1, frag_count, wait, 0)


def gather_kernel(frag_count, pot_ref, own_ref, all_ref, other_ref, wide, send_sem, recv_sem, orb_sems):
    greet(frag_count, True)
    finish = spread(frag_count, pot_ref, all_ref, send_sem, recv_sem)
    wide[...] = own_ref[...].astype(jnp.float32)
    swap = pltpu.make_async_remote_copy(
        src_ref=wide, dst_ref=other_ref, send_sem=orb_sems.at[0], recv_sem=orb_sems.at[1],
        **peer(orb=1 - lax.axis_index("orb")),
    )
    swap.start()
    all_ref[lax.axis_index("frag")] = pot_ref[...]
    finish()
    swap.wait()


def patch_kernel(frag_count, offsets_ref, signs_ref, assign_ref, rho_ref, out_ref, all_ref, send_sem, recv_sem):
    me = lax.axis_index("frag")
    greet(frag_count, False)
    finish = spread(frag_count, rho_ref, all_ref, send_sem, recv_sem)
    all_ref[me] = rho_ref[...]
    rows = lax.broadcasted_iota(jnp.int32, (PLANE, 2 * PLANE), 0)
    columns = lax.broadcasted_iota(jnp.int32, (PLANE, 2 * PLANE), 1)
    widen = (columns == 2 * rows - rows % FSIDE).astype(jnp.float32)
    finish()

    def add(d, sums):
        f = assign_ref[d]
        oz, ox, oy = offsets_ref[f, 0], offsets_ref[f, 1], offsets_ref[f, 2]
        half = lax.rem(me - oz // SLAB + frag_count, frag_count)
        sign = signs_ref[f].astype(jnp.float32) / NORB
        value = all_ref[d]
        lower = value[:SLAB] * jnp.where(half == 0, sign, 0.0)
        upper = value[SLAB:] * jnp.where(half == 1, sign, 0.0)
        both = lower + upper
        return tuple(
            sums[i] + both * jnp.where((ox == 8 * (i // 3)) & (oy == 8 * (i % 3)), 1.0, 0.0)
            for i in range(6)
        )

    sums = lax.fori_loop(0, frag_count, add, (jnp.zeros((SLAB, PLANE), jnp.float32),) * 6)
    wide = dot(jnp.concatenate(sums, axis=0), widen, ((1,), (0,)))
    out_ref[...] = jnp.zeros_like(out_ref)
    for i in range(6):
        part = wide[SLAB * i : SLAB * (i + 1)]
        if i % 3:
            part = pltpu.roll(part, 8 * (i % 3), 1)
        start = PLANE * (i // 3)
        out_ref[:, start : start + 2 * PLANE] += part


def local(potential, orbitals, offsets, weight_signs, assignment):
    frag_count = lax.axis_size("frag")
    own = orbitals[0]
    vmem = pl.BlockSpec(memory_space=pltpu.VMEM)
    smem = pl.BlockSpec(memory_space=pltpu.SMEM)
    sems = pltpu.SemaphoreType.DMA((frag_count - 1,))
    all_pot, other = pl.pallas_call(
        functools.partial(gather_kernel, frag_count),
        out_shape=(
            jax.ShapeDtypeStruct((frag_count,) + potential.shape, jnp.float32),
            jax.ShapeDtypeStruct(own.shape, jnp.float32),
        ),
        in_specs=[vmem, vmem],
        out_specs=(vmem, vmem),
        scratch_shapes=[pltpu.VMEM(own.shape, jnp.float32), sems, sems, pltpu.SemaphoreType.DMA((2,))],
        compiler_params=pltpu.CompilerParams(
            collective_id=0, has_side_effects=True, vmem_limit_bytes=24 * 1024 * 1024
        ),
    )(potential, own)
    states, rho = pl.pallas_call(
        fragment_kernel,
        out_shape=(
            jax.ShapeDtypeStruct((NORB, SLAB * PLANE), jnp.float32),
            jax.ShapeDtypeStruct((FSIDE, PLANE), jnp.float32),
        ),
        in_specs=[smem, smem, vmem, vmem, vmem],
        out_specs=(vmem, vmem),
        scratch_shapes=[
            pltpu.VMEM((PAD, PAD, ROWS, NORB), jnp.float32),
            pltpu.VMEM((PAD, PAD, ROWS, NORB), jnp.float32),
            pltpu.VMEM((FSIDE, FSIDE, FSIDE, NORB), jnp.float32),
            pltpu.VMEM((2, GX * GY, SLAB), jnp.float32),
            pltpu.VMEM((NORB, NORB), jnp.float32),
        ],
        compiler_params=pltpu.CompilerParams(vmem_limit_bytes=40 * 1024 * 1024),
    )(offsets, assignment, own, other, all_pot)
    density = pl.pallas_call(
        functools.partial(patch_kernel, frag_count),
        out_shape=jax.ShapeDtypeStruct((SLAB, GX * GY), jnp.float32),
        in_specs=[smem, smem, smem, vmem],
        out_specs=vmem,
        scratch_shapes=[pltpu.VMEM((frag_count, FSIDE, PLANE), jnp.float32), sems, sems],
        compiler_params=pltpu.CompilerParams(
            collective_id=1, has_side_effects=True, vmem_limit_bytes=24 * 1024 * 1024
        ),
    )(offsets, weight_signs, assignment, rho)
    return (density, states[None])


def solution(mesh):
    return jax.shard_map(
        local,
        mesh=mesh,
        in_specs=(
            P(("parts", "frag"), None),
            P(("parts", "frag"), None, "orb"),
            P("parts", None),
            P("parts"),
            P("parts"),
        ),
        out_specs=(P(("parts", "frag"), None), P(("parts", "frag"), None, "orb")),
        check_vma=False,
    )
```

```python
import functools

import jax
import jax.numpy as jnp
from jax import lax
from jax.experimental import pallas as pl
from jax.experimental.pallas import tpu as pltpu
from jax.sharding import PartitionSpec as P

NORB = 128
FSIDE = 16
DEGREE = 8
PASSES = 3
SLAB = 8
PLANE = 256
FCELLS = 4096
GX = 24
GY = 32
PAD = FSIDE + 2
ROWS = 32
LOW = 8
UNROLL = 4

SPECTRUM_MID = 3.5
SPECTRUM_HALF = 3.75
OCCUPY_SLOPE = 0.2
COUPLE = 1.0 / SPECTRUM_HALF
HIGHEST = lax.Precision.HIGHEST


def dot(left, right, dims):
    return lax.dot_general(
        left, right, (dims, ((), ())), precision=HIGHEST, preferred_element_type=jnp.float32
    )


def pieces(x):
    high = x.astype(jnp.bfloat16)
    return jnp.concatenate([high, (x - high.astype(jnp.float32)).astype(jnp.bfloat16)], axis=1)


def packed_dot(left, right, dims):
    return lax.dot_general(left, right, (dims, ((), ())), preferred_element_type=jnp.float32)


def quadrants(x):
    x = x[:NORB] + x[NORB:]
    return x[:, :NORB] + x[:, NORB:]


def twice(x):
    both = pieces(x)
    return jnp.concatenate([both, both], axis=0)


def inverse_factor(matrix):
    panels = NORB // 8
    lane = lax.broadcasted_iota(jnp.int32, (8, NORB), 1)
    sub = lax.broadcasted_iota(jnp.int32, (8, NORB), 0)
    a = [matrix[8 * i : 8 * i + 8] for i in range(panels)]
    w = [jnp.where(lane == sub + 8 * i, 1.0, 0.0).astype(jnp.float32) for i in range(panels)]
    out = []

    def row(x, j):
        return jnp.broadcast_to(x[j : j + 1], (8, NORB))

    for k in range(panels):
        cols = {
            i: [jnp.broadcast_to(a[i][:, 8 * k + j : 8 * k + j + 1], (8, NORB)) for j in range(8)]
            for i in range(k, panels)
        }
        scale = jnp.zeros((8, NORB), jnp.float32)
        for j in range(8):
            root = lax.rsqrt(row(cols[k][j], j))
            inv = root * root
            scale = jnp.where(sub == j, root, scale)
            col_rows = [row(cols[k][l], j) * inv for l in range(j + 1, 8)]
            a_row = row(a[k], j) * inv
            w_row = row(w[k], j) * inv
            for i in range(k, panels):
                f = cols[i][j]
                if i == k:
                    f = jnp.where(sub > j, f, 0.0)
                for l in range(j + 1, 8):
                    cols[i][l] = cols[i][l] - f * col_rows[l - j - 1]
                a[i] = a[i] - f * a_row
                w[i] = w[i] - f * w_row
        out.append(w[k] * scale)
    return jnp.concatenate(out, axis=0)


def fragment_kernel(
    offsets_ref, assign_ref, own_ref, other_ref, pot_ref, states_ref, rho_ref, xa, xb, v_ref, turned, w_ref
):
    orb = lax.axis_index("orb")
    frag_count = pot_ref.shape[0]
    f = assign_ref[lax.axis_index("frag")]
    oz, ox, oy = offsets_ref[f, 0], offsets_ref[f, 1], offsets_ref[f, 2]
    for half in range(2):
        slab = pot_ref[lax.rem(oz // SLAB + half, frag_count)]
        turned[half] = ((slab + (3.0 - SPECTRUM_MID)) * (2.0 / SPECTRUM_HALF)).T
    for half in range(2):
        for x in range(FSIDE):
            cells = turned[half, pl.ds(pl.multiple_of((ox + x) * GY + oy, 8), FSIDE), :]
            for z in range(SLAB):
                v_ref[half * SLAB + z, x] = jnp.broadcast_to(cells[:, z : z + 1], (FSIDE, NORB))

    def clear(z, _):
        xa[z] = jnp.zeros((PAD, ROWS, NORB), jnp.float32)
        xb[z] = jnp.zeros((PAD, ROWS, NORB), jnp.float32)
        return 0

    lax.fori_loop(0, PAD, clear, 0)

    for z in range(SLAB):
        block = own_ref[:, PLANE * z : PLANE * (z + 1)].astype(jnp.float32).T
        xa[orb * SLAB + z + 1, 1 : FSIDE + 1, LOW : LOW + FSIDE, :] = block.reshape(FSIDE, FSIDE, NORB)
        block = other_ref[:, PLANE * z : PLANE * (z + 1)].T
        xa[(1 - orb) * SLAB + z + 1, 1 : FSIDE + 1, LOW : LOW + FSIDE, :] = block.reshape(FSIDE, FSIDE, NORB)

    mid = pl.ds(LOW, FSIDE)

    def sweep(src, planes, z0, emit):
        held = {}

        def at(k, x):
            if (k, x) not in held:
                held[k, x] = src[z0 + k, x, mid, :]
            return held[k, x]

        for x in range(FSIDE):
            for k in range(planes):
                c = at(k + 1, x + 1)
                n = at(k, x + 1) + at(k + 2, x + 1)
                n = n + (at(k + 1, x) + at(k + 1, x + 2))
                n = n + (
                    src[z0 + k + 1, x + 1, pl.ds(LOW - 1, FSIDE), :]
                    + src[z0 + k + 1, x + 1, pl.ds(LOW + 1, FSIDE), :]
                )
                emit(k, x, v_ref[z0 + k, x] * c - COUPLE * n, c)

    def first(src, dst):
        def body(i, _):
            def emit(k, x, value, c):
                dst[UNROLL * i + k + 1, x + 1, mid, :] = 0.5 * value

            sweep(src, UNROLL, UNROLL * i, emit)
            return 0

        lax.fori_loop(0, FSIDE // UNROLL, body, 0)

    def later(src, dst):
        def body(i, _):
            def emit(k, x, value, c):
                z = UNROLL * i + k + 1
                dst[z, x + 1, mid, :] = value - dst[z, x + 1, mid, :]

            sweep(src, UNROLL, UNROLL * i, emit)
            return 0

        lax.fori_loop(0, FSIDE // UNROLL, body, 0)

    def plane(src, z):
        return src[z + 1, 1 : FSIDE + 1, mid, :].reshape(PLANE, NORB)

    def one_pass(_, carry):
        first(xa, xb)
        later(xb, xa)

        def pair(_, c):
            later(xa, xb)
            later(xb, xa)
            return c

        lax.fori_loop(0, DEGREE // 2 - 1, pair, 0)

        def add(z, total):
            y = pieces(plane(xa, z))
            return total + packed_dot(y, y, ((0,), (0,)))

        total = lax.fori_loop(0, FSIDE, add, jnp.zeros((2 * NORB, 2 * NORB), jnp.float32), unroll=2)
        w_ref[...] = twice(inverse_factor(quadrants(total) / FCELLS).T)

        def apply(z, c):
            s = packed_dot(pieces(plane(xa, z)), w_ref[...], ((1,), (0,)))
            s = s[:, :NORB] + s[:, NORB:]
            xa[z + 1, 1 : FSIDE + 1, mid, :] = s.reshape(FSIDE, FSIDE, NORB)
            return c

        lax.fori_loop(0, FSIDE, apply, 0, unroll=2)
        return carry

    lax.fori_loop(0, PASSES, one_pass, 0)

    def couple(z, total):
        parts = []
        sweep(
            xa, 1, z, lambda k, x, value, c: parts.append((SPECTRUM_HALF / 2) * value + SPECTRUM_MID * c)
        )
        h = jnp.concatenate(parts, axis=0)
        return total + packed_dot(pieces(plane(xa, z)), pieces(h), ((0,), (0,)))

    total = lax.fori_loop(0, FSIDE, couple, jnp.zeros((2 * NORB, 2 * NORB), jnp.float32))
    coupling = quadrants(total) / FCELLS
    projected = 0.5 * (coupling + coupling.T)
    rows = lax.broadcasted_iota(jnp.int32, (NORB, NORB), 0)
    columns = lax.broadcasted_iota(jnp.int32, (NORB, NORB), 1)
    eye = jnp.where(rows == columns, 1.0, 0.0).astype(jnp.float32)
    trace = jnp.sum(projected * eye)
    occupied = 0.5 * eye - OCCUPY_SLOPE * (projected - trace / NORB * eye)
    for _ in range(2):
        square = dot(occupied, occupied, ((1,), (0,)))
        cube = dot(square, occupied, ((1,), (0,)))
        occupied = 3.0 * square - 2.0 * cube
    w_ref[...] = twice(occupied)
    ones = jnp.ones((8, 2 * NORB), jnp.bfloat16)

    def density(z, c):
        s = plane(xa, z)
        m = packed_dot(pieces(s), w_ref[...], ((1,), (0,)))
        m = s * (m[:, :NORB] + m[:, NORB:])
        r = packed_dot(ones, pieces(m), ((1,), (1,)))
        rho_ref[pl.ds(z, 1), :] = r[0:1]
        return c

    lax.fori_loop(0, FSIDE, density, 0, unroll=2)
    for z in range(SLAB):
        states_ref[:, PLANE * z : PLANE * (z + 1)] = plane(xa, orb * SLAB + z).T


def peer(**where):
    return {"device_id": where, "device_id_type": pl.DeviceIdType.MESH}


def greet(frag_count, with_orb):
    me, orb = lax.axis_index("frag"), lax.axis_index("orb")
    barrier = pltpu.get_barrier_semaphore()

    def hello(i, c):
        pl.semaphore_signal(barrier, inc=1, **peer(frag=lax.rem(me + i, frag_count)))
        return c

    lax.fori_loop(1, frag_count, hello, 0)
    if with_orb:
        pl.semaphore_signal(barrier, inc=1, **peer(orb=1 - orb))
    pl.semaphore_wait(barrier, frag_count - 1 + int(with_orb))


def spread(frag_count, source, gathered, send_sem, recv_sem):
    me = lax.axis_index("frag")

    def copy_to(i):
        return pltpu.make_async_remote_copy(
            src_ref=source,
            dst_ref=gathered.at[me],
            send_sem=send_sem.at[i - 1],
            recv_sem=recv_sem.at[i - 1],
            **peer(frag=lax.rem(me + i, frag_count)),
        )

    def start(i, c):
        copy_to(i).start()
        return c

    def wait(i, c):
        copy_to(i).wait()
        return c

    lax.fori_loop(1, frag_count, start, 0)
    return lambda: lax.fori_loop(1, frag_count, wait, 0)


def gather_kernel(frag_count, pot_ref, own_ref, all_ref, other_ref, wide, send_sem, recv_sem, orb_sems):
    greet(frag_count, True)
    finish = spread(frag_count, pot_ref, all_ref, send_sem, recv_sem)
    wide[...] = own_ref[...].astype(jnp.float32)
    swap = pltpu.make_async_remote_copy(
        src_ref=wide, dst_ref=other_ref, send_sem=orb_sems.at[0], recv_sem=orb_sems.at[1],
        **peer(orb=1 - lax.axis_index("orb")),
    )
    swap.start()
    all_ref[lax.axis_index("frag")] = pot_ref[...]
    finish()
    swap.wait()


def patch_kernel(frag_count, offsets_ref, signs_ref, assign_ref, rho_ref, out_ref, all_ref, send_sem, recv_sem):
    me = lax.axis_index("frag")
    greet(frag_count, False)
    finish = spread(frag_count, rho_ref, all_ref, send_sem, recv_sem)
    all_ref[me] = rho_ref[...]
    rows = lax.broadcasted_iota(jnp.int32, (PLANE, 2 * PLANE), 0)
    columns = lax.broadcasted_iota(jnp.int32, (PLANE, 2 * PLANE), 1)
    widen = (columns == 2 * rows - rows % FSIDE).astype(jnp.float32)
    finish()

    def add(d, sums):
        f = assign_ref[d]
        oz, ox, oy = offsets_ref[f, 0], offsets_ref[f, 1], offsets_ref[f, 2]
        half = lax.rem(me - oz // SLAB + frag_count, frag_count)
        sign = signs_ref[f].astype(jnp.float32) / NORB
        value = all_ref[d]
        lower = value[:SLAB] * jnp.where(half == 0, sign, 0.0)
        upper = value[SLAB:] * jnp.where(half == 1, sign, 0.0)
        both = lower + upper
        return tuple(
            sums[i] + both * jnp.where((ox == 8 * (i // 3)) & (oy == 8 * (i % 3)), 1.0, 0.0)
            for i in range(6)
        )

    sums = lax.fori_loop(0, frag_count, add, (jnp.zeros((SLAB, PLANE), jnp.float32),) * 6)
    wide = dot(jnp.concatenate(sums, axis=0), widen, ((1,), (0,)))
    out_ref[...] = jnp.zeros_like(out_ref)
    for i in range(6):
        part = wide[SLAB * i : SLAB * (i + 1)]
        if i % 3:
            part = pltpu.roll(part, 8 * (i % 3), 1)
        start = PLANE * (i // 3)
        out_ref[:, start : start + 2 * PLANE] += part


def local(potential, orbitals, offsets, weight_signs, assignment):
    frag_count = lax.axis_size("frag")
    own = orbitals[0]
    vmem = pl.BlockSpec(memory_space=pltpu.VMEM)
    smem = pl.BlockSpec(memory_space=pltpu.SMEM)
    sems = pltpu.SemaphoreType.DMA((frag_count - 1,))
    all_pot, other = pl.pallas_call(
        functools.partial(gather_kernel, frag_count),
        out_shape=(
            jax.ShapeDtypeStruct((frag_count,) + potential.shape, jnp.float32),
            jax.ShapeDtypeStruct(own.shape, jnp.float32),
        ),
        in_specs=[vmem, vmem],
        out_specs=(vmem, vmem),
        scratch_shapes=[pltpu.VMEM(own.shape, jnp.float32), sems, sems, pltpu.SemaphoreType.DMA((2,))],
        compiler_params=pltpu.CompilerParams(
            collective_id=0, has_side_effects=True, vmem_limit_bytes=24 * 1024 * 1024
        ),
    )(potential, own)
    states, rho = pl.pallas_call(
        fragment_kernel,
        out_shape=(
            jax.ShapeDtypeStruct((NORB, SLAB * PLANE), jnp.float32),
            jax.ShapeDtypeStruct((FSIDE, PLANE), jnp.float32),
        ),
        in_specs=[smem, smem, vmem, vmem, vmem],
        out_specs=(vmem, vmem),
        scratch_shapes=[
            pltpu.VMEM((PAD, PAD, ROWS, NORB), jnp.float32),
            pltpu.VMEM((PAD, PAD, ROWS, NORB), jnp.float32),
            pltpu.VMEM((FSIDE, FSIDE, FSIDE, NORB), jnp.float32),
            pltpu.VMEM((2, GX * GY, SLAB), jnp.float32),
            pltpu.VMEM((2 * NORB, 2 * NORB), jnp.bfloat16),
        ],
        compiler_params=pltpu.CompilerParams(vmem_limit_bytes=40 * 1024 * 1024),
    )(offsets, assignment, own, other, all_pot)
    density = pl.pallas_call(
        functools.partial(patch_kernel, frag_count),
        out_shape=jax.ShapeDtypeStruct((SLAB, GX * GY), jnp.float32),
        in_specs=[smem, smem, smem, vmem],
        out_specs=vmem,
        scratch_shapes=[pltpu.VMEM((frag_count, FSIDE, PLANE), jnp.float32), sems, sems],
        compiler_params=pltpu.CompilerParams(
            collective_id=1, has_side_effects=True, vmem_limit_bytes=24 * 1024 * 1024
        ),
    )(offsets, weight_signs, assignment, rho)
    return (density, states[None])


def solution(mesh):
    return jax.shard_map(
        local,
        mesh=mesh,
        in_specs=(
            P(("parts", "frag"), None),
            P(("parts", "frag"), None, "orb"),
            P("parts", None),
            P("parts"),
            P("parts"),
        ),
        out_specs=(P(("parts", "frag"), None), P(("parts", "frag"), None, "orb")),
        check_vma=False,
    )
```

```python
import functools

import jax
import jax.numpy as jnp
from jax import lax
from jax.experimental import pallas as pl
from jax.experimental.pallas import tpu as pltpu
from jax.sharding import PartitionSpec as P

NORB = 128
FSIDE = 16
DEGREE = 8
PASSES = 3
SLAB = 8
PLANE = 256
FCELLS = 4096
GX = 24
GY = 32
PAD = FSIDE + 2
ROWS = 32
LOW = 8
UNROLL = 4
CHUNKS = 4

SPECTRUM_MID = 3.5
SPECTRUM_HALF = 3.75
OCCUPY_SLOPE = 0.2
COUPLE = 1.0 / SPECTRUM_HALF
HIGHEST = lax.Precision.HIGHEST


def dot(left, right, dims):
    return lax.dot_general(
        left, right, (dims, ((), ())), precision=HIGHEST, preferred_element_type=jnp.float32
    )


def pieces(x):
    high = x.astype(jnp.bfloat16)
    return jnp.concatenate([high, (x - high.astype(jnp.float32)).astype(jnp.bfloat16)], axis=1)


def packed_dot(left, right, dims):
    return lax.dot_general(left, right, (dims, ((), ())), preferred_element_type=jnp.float32)


def quadrants(x):
    x = x[:NORB] + x[NORB:]
    return x[:, :NORB] + x[:, NORB:]


def twice(x):
    both = pieces(x)
    return jnp.concatenate([both, both], axis=0)


def inverse_factor(matrix):
    panels = NORB // 8
    lane = lax.broadcasted_iota(jnp.int32, (8, NORB), 1)
    sub = lax.broadcasted_iota(jnp.int32, (8, NORB), 0)
    a = [matrix[8 * i : 8 * i + 8] for i in range(panels)]
    w = [jnp.where(lane == sub + 8 * i, 1.0, 0.0).astype(jnp.float32) for i in range(panels)]
    out = []

    def row(x, j):
        return jnp.broadcast_to(x[j : j + 1], (8, NORB))

    for k in range(panels):
        cols = {
            i: [jnp.broadcast_to(a[i][:, 8 * k + j : 8 * k + j + 1], (8, NORB)) for j in range(8)]
            for i in range(k, panels)
        }
        scale = jnp.zeros((8, NORB), jnp.float32)
        for j in range(8):
            root = lax.rsqrt(row(cols[k][j], j))
            inv = root * root
            scale = jnp.where(sub == j, root, scale)
            col_rows = [row(cols[k][l], j) * inv for l in range(j + 1, 8)]
            a_row = row(a[k], j) * inv
            w_row = row(w[k], j) * inv
            for i in range(k, panels):
                f = cols[i][j]
                if i == k:
                    f = jnp.where(sub > j, f, 0.0)
                for l in range(j + 1, 8):
                    cols[i][l] = cols[i][l] - f * col_rows[l - j - 1]
                a[i] = a[i] - f * a_row
                w[i] = w[i] - f * w_row
        out.append(w[k] * scale)
    return jnp.concatenate(out, axis=0)


def fragment_kernel(
    offsets_ref, assign_ref, own_ref, other_ref, pot_ref, states_ref, rho_ref, xa, xb, v_ref, turned, w_ref
):
    orb = lax.axis_index("orb")
    frag_count = pot_ref.shape[0]
    f = assign_ref[lax.axis_index("frag")]
    oz, ox, oy = offsets_ref[f, 0], offsets_ref[f, 1], offsets_ref[f, 2]
    for half in range(2):
        slab = pot_ref[lax.rem(oz // SLAB + half, frag_count)]
        turned[half] = ((slab + (3.0 - SPECTRUM_MID)) * (2.0 / SPECTRUM_HALF)).T
    for half in range(2):
        for x in range(FSIDE):
            cells = turned[half, pl.ds(pl.multiple_of((ox + x) * GY + oy, 8), FSIDE), :]
            for z in range(SLAB):
                v_ref[half * SLAB + z, x] = jnp.broadcast_to(cells[:, z : z + 1], (FSIDE, NORB))

    for ref in (xa, xb):
        for z in (0, PAD - 1):
            ref[z] = jnp.zeros((PAD, ROWS, NORB), jnp.float32)

    def clear(z, _):
        for ref in (xa, xb):
            for x in (0, PAD - 1):
                ref[z, x] = jnp.zeros((ROWS, NORB), jnp.float32)
            ref[z, :, 0:LOW, :] = jnp.zeros((PAD, LOW, NORB), jnp.float32)
            ref[z, :, LOW + FSIDE : ROWS, :] = jnp.zeros((PAD, LOW, NORB), jnp.float32)
        return 0

    lax.fori_loop(1, PAD - 1, clear, 0)

    for z in range(SLAB):
        block = own_ref[:, PLANE * z : PLANE * (z + 1)].astype(jnp.float32).T
        xa[orb * SLAB + z + 1, 1 : FSIDE + 1, LOW : LOW + FSIDE, :] = block.reshape(FSIDE, FSIDE, NORB)
        block = other_ref[:, PLANE * z : PLANE * (z + 1)].T
        xa[(1 - orb) * SLAB + z + 1, 1 : FSIDE + 1, LOW : LOW + FSIDE, :] = block.reshape(FSIDE, FSIDE, NORB)

    mid = pl.ds(LOW, FSIDE)

    def sweep(src, planes, z0, emit):
        held = {}

        def at(k, x):
            if (k, x) not in held:
                held[k, x] = src[z0 + k, x, mid, :]
            return held[k, x]

        for x in range(FSIDE):
            for k in range(planes):
                c = at(k + 1, x + 1)
                n = at(k, x + 1) + at(k + 2, x + 1)
                n = n + (at(k + 1, x) + at(k + 1, x + 2))
                n = n + (
                    src[z0 + k + 1, x + 1, pl.ds(LOW - 1, FSIDE), :]
                    + src[z0 + k + 1, x + 1, pl.ds(LOW + 1, FSIDE), :]
                )
                emit(k, x, v_ref[z0 + k, x] * c - COUPLE * n, c)

    def first(src, dst):
        def body(i, _):
            def emit(k, x, value, c):
                dst[UNROLL * i + k + 1, x + 1, mid, :] = 0.5 * value

            sweep(src, UNROLL, UNROLL * i, emit)
            return 0

        lax.fori_loop(0, FSIDE // UNROLL, body, 0)

    def later(src, dst):
        def body(i, _):
            def emit(k, x, value, c):
                z = UNROLL * i + k + 1
                dst[z, x + 1, mid, :] = value - dst[z, x + 1, mid, :]

            sweep(src, UNROLL, UNROLL * i, emit)
            return 0

        lax.fori_loop(0, FSIDE // UNROLL, body, 0)

    def plane(src, z):
        return src[z + 1, 1 : FSIDE + 1, mid, :].reshape(PLANE, NORB)

    def one_pass(_, carry):
        first(xa, xb)
        later(xb, xa)

        def pair(_, c):
            later(xa, xb)
            later(xb, xa)
            return c

        lax.fori_loop(0, DEGREE // 2 - 1, pair, 0)

        def add(z, total):
            y = pieces(plane(xa, z))
            return total + packed_dot(y, y, ((0,), (0,)))

        total = lax.fori_loop(0, FSIDE, add, jnp.zeros((2 * NORB, 2 * NORB), jnp.float32), unroll=4)
        w_ref[...] = twice(inverse_factor(quadrants(total) / FCELLS).T)

        def apply(z, c):
            s = packed_dot(pieces(plane(xa, z)), w_ref[...], ((1,), (0,)))
            s = s[:, :NORB] + s[:, NORB:]
            xa[z + 1, 1 : FSIDE + 1, mid, :] = s.reshape(FSIDE, FSIDE, NORB)
            return c

        lax.fori_loop(0, FSIDE, apply, 0, unroll=4)
        return carry

    lax.fori_loop(0, PASSES, one_pass, 0)

    def couple(z, total):
        parts = []
        sweep(
            xa, 1, z, lambda k, x, value, c: parts.append((SPECTRUM_HALF / 2) * value + SPECTRUM_MID * c)
        )
        h = jnp.concatenate(parts, axis=0)
        return total + packed_dot(pieces(plane(xa, z)), pieces(h), ((0,), (0,)))

    total = lax.fori_loop(0, FSIDE, couple, jnp.zeros((2 * NORB, 2 * NORB), jnp.float32))
    coupling = quadrants(total) / FCELLS
    projected = 0.5 * (coupling + coupling.T)
    rows = lax.broadcasted_iota(jnp.int32, (NORB, NORB), 0)
    columns = lax.broadcasted_iota(jnp.int32, (NORB, NORB), 1)
    eye = jnp.where(rows == columns, 1.0, 0.0).astype(jnp.float32)
    trace = jnp.sum(projected * eye)
    occupied = 0.5 * eye - OCCUPY_SLOPE * (projected - trace / NORB * eye)
    for _ in range(2):
        square = dot(occupied, occupied, ((1,), (0,)))
        cube = dot(square, occupied, ((1,), (0,)))
        occupied = 3.0 * square - 2.0 * cube
    w_ref[...] = twice(occupied)
    ones = jnp.ones((8, 2 * NORB), jnp.bfloat16)

    def density(z, c):
        s = plane(xa, z)
        m = packed_dot(pieces(s), w_ref[...], ((1,), (0,)))
        m = s * (m[:, :NORB] + m[:, NORB:])
        r = packed_dot(ones, pieces(m), ((1,), (1,)))
        rho_ref[pl.ds(z, 1), :] = r[0:1]
        return c

    lax.fori_loop(0, FSIDE, density, 0, unroll=4)
    for z in range(SLAB):
        states_ref[:, PLANE * z : PLANE * (z + 1)] = plane(xa, orb * SLAB + z).T


def peer(**where):
    return {"device_id": where, "device_id_type": pl.DeviceIdType.MESH}


def greet(frag_count, with_orb):
    me, orb = lax.axis_index("frag"), lax.axis_index("orb")
    barrier = pltpu.get_barrier_semaphore()

    def hello(i, c):
        pl.semaphore_signal(barrier, inc=1, **peer(frag=lax.rem(me + i, frag_count)))
        return c

    lax.fori_loop(1, frag_count, hello, 0)
    if with_orb:
        pl.semaphore_signal(barrier, inc=1, **peer(orb=1 - orb))
    pl.semaphore_wait(barrier, frag_count - 1 + int(with_orb))


def spread(frag_count, source, gathered, send_sem, recv_sem):
    me = lax.axis_index("frag")

    def copy_to(i):
        return pltpu.make_async_remote_copy(
            src_ref=source,
            dst_ref=gathered.at[me],
            send_sem=send_sem.at[i - 1],
            recv_sem=recv_sem.at[i - 1],
            **peer(frag=lax.rem(me + i, frag_count)),
        )

    def start(i, c):
        copy_to(i).start()
        return c

    def wait(i, c):
        copy_to(i).wait()
        return c

    lax.fori_loop(1, frag_count, start, 0)
    return lambda: lax.fori_loop(1, frag_count, wait, 0)


def gather_kernel(frag_count, pot_ref, own_ref, all_ref, other_ref, wide, send_sem, recv_sem, orb_sems):
    greet(frag_count, True)
    finish = spread(frag_count, pot_ref, all_ref, send_sem, recv_sem)
    other = 1 - lax.axis_index("orb")
    swaps = []
    for i in range(CHUNKS):
        part = pl.ds(i * (NORB // CHUNKS), NORB // CHUNKS)
        wide[part, :] = own_ref[part, :].astype(jnp.float32)
        swaps.append(
            pltpu.make_async_remote_copy(
                src_ref=wide.at[part, :], dst_ref=other_ref.at[part, :],
                send_sem=orb_sems.at[0, i], recv_sem=orb_sems.at[1, i], **peer(orb=other),
            )
        )
        swaps[-1].start()
    all_ref[lax.axis_index("frag")] = pot_ref[...]
    finish()
    for swap in swaps:
        swap.wait()


def patch_kernel(frag_count, offsets_ref, signs_ref, assign_ref, rho_ref, out_ref, all_ref, send_sem, recv_sem):
    me = lax.axis_index("frag")
    greet(frag_count, False)
    finish = spread(frag_count, rho_ref, all_ref, send_sem, recv_sem)
    all_ref[me] = rho_ref[...]
    rows = lax.broadcasted_iota(jnp.int32, (PLANE, 2 * PLANE), 0)
    columns = lax.broadcasted_iota(jnp.int32, (PLANE, 2 * PLANE), 1)
    widen = jnp.where(columns == 2 * rows - rows % FSIDE, 1.0, 0.0).astype(jnp.bfloat16)
    finish()

    def add(d, sums):
        f = assign_ref[d]
        oz, ox, oy = offsets_ref[f, 0], offsets_ref[f, 1], offsets_ref[f, 2]
        half = lax.rem(me - oz // SLAB + frag_count, frag_count)
        sign = signs_ref[f].astype(jnp.float32) / NORB
        value = all_ref[d]
        lower = value[:SLAB] * jnp.where(half == 0, sign, 0.0)
        upper = value[SLAB:] * jnp.where(half == 1, sign, 0.0)
        both = lower + upper
        return tuple(
            sums[i] + both * jnp.where((ox == 8 * (i // 3)) & (oy == 8 * (i % 3)), 1.0, 0.0)
            for i in range(6)
        )

    sums = lax.fori_loop(0, frag_count, add, (jnp.zeros((SLAB, PLANE), jnp.float32),) * 6)
    sums = jnp.concatenate(sums, axis=0)
    high = sums.astype(jnp.bfloat16)
    rest = (sums - high.astype(jnp.float32)).astype(jnp.bfloat16)
    wide = packed_dot(high, widen, ((1,), (0,))) + packed_dot(rest, widen, ((1,), (0,)))
    out_ref[...] = jnp.zeros_like(out_ref)
    for i in range(6):
        part = wide[SLAB * i : SLAB * (i + 1)]
        if i % 3:
            part = pltpu.roll(part, 8 * (i % 3), 1)
        start = PLANE * (i // 3)
        out_ref[:, start : start + 2 * PLANE] += part


def local(potential, orbitals, offsets, weight_signs, assignment):
    frag_count = lax.axis_size("frag")
    own = orbitals[0]
    vmem = pl.BlockSpec(memory_space=pltpu.VMEM)
    smem = pl.BlockSpec(memory_space=pltpu.SMEM)
    sems = pltpu.SemaphoreType.DMA((frag_count - 1,))
    all_pot, other = pl.pallas_call(
        functools.partial(gather_kernel, frag_count),
        out_shape=(
            jax.ShapeDtypeStruct((frag_count,) + potential.shape, jnp.float32),
            jax.ShapeDtypeStruct(own.shape, jnp.float32),
        ),
        in_specs=[vmem, vmem],
        out_specs=(vmem, vmem),
        scratch_shapes=[pltpu.VMEM(own.shape, jnp.float32), sems, sems, pltpu.SemaphoreType.DMA((2, CHUNKS))],
        compiler_params=pltpu.CompilerParams(
            collective_id=0, has_side_effects=True, vmem_limit_bytes=24 * 1024 * 1024
        ),
    )(potential, own)
    states, rho = pl.pallas_call(
        fragment_kernel,
        out_shape=(
            jax.ShapeDtypeStruct((NORB, SLAB * PLANE), jnp.float32),
            jax.ShapeDtypeStruct((FSIDE, PLANE), jnp.float32),
        ),
        in_specs=[smem, smem, vmem, vmem, vmem],
        out_specs=(vmem, vmem),
        scratch_shapes=[
            pltpu.VMEM((PAD, PAD, ROWS, NORB), jnp.float32),
            pltpu.VMEM((PAD, PAD, ROWS, NORB), jnp.float32),
            pltpu.VMEM((FSIDE, FSIDE, FSIDE, NORB), jnp.float32),
            pltpu.VMEM((2, GX * GY, SLAB), jnp.float32),
            pltpu.VMEM((2 * NORB, 2 * NORB), jnp.bfloat16),
        ],
        compiler_params=pltpu.CompilerParams(vmem_limit_bytes=40 * 1024 * 1024),
    )(offsets, assignment, own, other, all_pot)
    density = pl.pallas_call(
        functools.partial(patch_kernel, frag_count),
        out_shape=jax.ShapeDtypeStruct((SLAB, GX * GY), jnp.float32),
        in_specs=[smem, smem, smem, vmem],
        out_specs=vmem,
        scratch_shapes=[pltpu.VMEM((frag_count, FSIDE, PLANE), jnp.float32), sems, sems],
        compiler_params=pltpu.CompilerParams(
            collective_id=1, has_side_effects=True, vmem_limit_bytes=24 * 1024 * 1024
        ),
    )(offsets, weight_signs, assignment, rho)
    return (density, states[None])


def solution(mesh):
    return jax.shard_map(
        local,
        mesh=mesh,
        in_specs=(
            P(("parts", "frag"), None),
            P(("parts", "frag"), None, "orb"),
            P("parts", None),
            P("parts"),
            P("parts"),
        ),
        out_specs=(P(("parts", "frag"), None), P(("parts", "frag"), None, "orb")),
        check_vma=False,
    )
```
